32 devices in a mesh: row: 16 (over z, x, core), col: 2 (over y).
Axes of the slice: x: 2, y: 2, z: 4, core: 2. Of those that a mesh axis runs over, the one named last changes fastest.
Arguments:
- blocks: bfloat16 [16, 64, 128, 128], P('row', 'col')
- block_rows: int32 [16, 64], P('row', 'col'), may hold values from 0 to 31, as said below
- block_cols: int32 [16, 64], P('row', 'col'), may hold values from 0 to 31, as said below
- counts: int32 [16, 2], P('row', 'col'), may hold values from 1 to 32, as said below
- trials: bfloat16 [4096, 256], P(('col', 'row')), may hold values from -6 to 6
Outputs:
- basis: float32 [4096, 256], P(('col', 'row'))
- factor: float32 [256, 256], replicated
The draws below stay inside these ranges and needn't reach their ends.
Inputs may be any that keep to these rules, and one draw needn't show every extreme that they name: The live slots of a device are its first counts[r, c] slots, and at least one device has all 32 slots live. `block_rows`: for the device at grid position (r, c), every slot's block row leaves remainder r on division by the size of axis row. The live slots of a device name distinct blocks with block row at most block column; slots past the count hold arbitrary blocks whose coordinates have the same form. `block_cols`: for the device at grid position (r, c), every slot's block column divided by the size of axis row gives c.
All inputs are finite; a program needn't handle non-finite values.
Results may differ from the reference program's by a relative error of at most 0.0003.
Values may be sent and summed in bfloat16 or wider, within the bound.
A program may use at most 64 MiB of HBM per device.

```python
import jax
import jax.numpy as jnp
from jax import lax

BS = 128
K = 256
SLOTS = 32
NW = 4096
N_ROW = 16
N_COL = 2


def block_layout(key):
    base_key = jax.random.fold_in(key, 4021)
    score_key, load_key, pick_key = jax.random.split(base_key, 3)
    tile_size = N_ROW * N_COL
    grid_row = jnp.arange(N_ROW, dtype=jnp.int32)[:, None, None]
    grid_col = jnp.arange(N_COL, dtype=jnp.int32)[None, :, None]
    places = jnp.arange(tile_size, dtype=jnp.int32)[None, None, :]
    row_index = places // N_ROW * N_ROW + grid_row
    col_index = grid_col * N_ROW + places % N_ROW
    allowed = row_index <= col_index
    scores = jax.random.randint(score_key, (N_ROW, N_COL, tile_size), 0, 1 << 20) * tile_size + places
    scores = jnp.where(allowed, scores, scores + (1 << 29))
    order = jnp.argsort(scores, axis=-1)[:, :, :SLOTS].astype(jnp.int32)
    row_full = jnp.broadcast_to(row_index, scores.shape)
    col_full = jnp.broadcast_to(col_index, scores.shape)
    row_pick = jnp.take_along_axis(row_full, order, axis=-1)
    col_pick = jnp.take_along_axis(col_full, order, axis=-1)
    room = grid_col[:, :, 0] * N_ROW + N_ROW - grid_row[:, :, 0]
    loads = jax.random.randint(load_key, (N_ROW, N_COL), 1, 2 * SLOTS // 3 + 1)
    loads = jnp.minimum(loads, room)
    full_row = jax.random.randint(pick_key, (), 0, min(N_ROW, N_ROW * N_COL - SLOTS + 1))
    forced = (jnp.arange(N_ROW, dtype=jnp.int32)[:, None] == full_row) & (jnp.arange(N_COL, dtype=jnp.int32)[None, :] == N_COL - 1)
    loads = jnp.where(forced, SLOTS, loads).astype(jnp.int32)
    return (row_pick.reshape(N_ROW, N_COL * SLOTS), col_pick.reshape(N_ROW, N_COL * SLOTS), loads)


def draw_block_rows(key, part):
    return block_layout(key)[0]


def draw_block_cols(key, part):
    return block_layout(key)[1]


def draw_counts(key, part):
    return block_layout(key)[2]


def draw_blocks(key, part):
    row_pick, col_pick, loads = block_layout(key)
    base_key, rough_key = jax.random.split(jax.random.fold_in(key, 977), 2)
    shape = (N_ROW, N_COL * SLOTS, BS, BS)
    base = jax.random.normal(base_key, shape, jnp.float32)
    places = jnp.arange(N_ROW * N_COL, dtype=jnp.int32)
    rough = jnp.exp(jax.random.uniform(rough_key, (N_ROW * N_COL,), jnp.float32, -0.69, 0.69))
    profile = jnp.exp(0.55 * (2.0 * (places % N_ROW).astype(jnp.float32) / (N_ROW - 1) - 1.0)) * rough
    amplitude = profile[row_pick] * profile[col_pick]
    return (base * amplitude[:, :, None, None] * (BS * SLOTS) ** (-0.5)).astype(jnp.bfloat16)


def block_levels(key, dims, cuts, low, high):
    level, own = 1.0, jax.random.fold_in(key, 6)
    for position, shards_of in cuts:
        steps = jnp.exp(jax.random.uniform(jax.random.fold_in(own, position), (shards_of,), jnp.float32, low / len(cuts), high / len(cuts)))
        level = level * jnp.repeat(steps, dims[position] // shards_of).reshape([-1 if axis == position else 1 for axis in range(len(dims))])
    return level


def bell_draw(rng, extent, spread, bound, cuts=(), kind=jnp.bfloat16):
    drawn = jax.random.normal(rng, extent, jnp.float32) * spread
    if len(cuts) > 0:
        drawn = block_levels(rng, extent, cuts, -0.22, 0.18) * drawn
    return jnp.clip(drawn, min=-bound, max=bound).astype(kind)


def setup_inputs(seed: int = 0) -> dict:
    key_of = jax.random.split(jax.random.key(seed), 6)
    return {
        "blocks": draw_blocks(jax.random.fold_in(key_of[5], 71), 0),
        "block_rows": draw_block_rows(jax.random.fold_in(key_of[5], 71), 0),
        "block_cols": draw_block_cols(jax.random.fold_in(key_of[5], 71), 0),
        "counts": draw_counts(jax.random.fold_in(key_of[5], 71), 0),
        "trials": bell_draw(key_of[4], (NW, K), 1.0, 6.0, ((0, 32),)),
    }


def reference(blocks, block_rows, block_cols, counts, trials):
    total = N_ROW * N_COL
    flat_blocks = blocks.reshape(total * SLOTS, BS, BS)
    flat_rows = block_rows.reshape(total * SLOTS).astype(jnp.int32)
    flat_cols = block_cols.reshape(total * SLOTS).astype(jnp.int32)
    positions = jnp.arange(SLOTS, dtype=jnp.int32)[None, None, :]
    alive = (positions < counts[:, :, None]).reshape(total * SLOTS)
    weights = jnp.where(alive, jnp.where(flat_rows == flat_cols, 0.5, 1.0), 0.0).astype(jnp.float32)
    vectors = trials.reshape(total, BS, K)

    def add_block(accum, item):
        tile, row_at, col_at, weight = item

        def apply_block(inner):
            direct = jnp.dot(tile.astype(jnp.float32), vectors[col_at].astype(jnp.float32), preferred_element_type=jnp.float32)
            mirror = jnp.dot(tile.T.astype(jnp.float32), vectors[row_at].astype(jnp.float32), preferred_element_type=jnp.float32)
            inner = inner.at[row_at].add(weight * direct)
            return inner.at[col_at].add(weight * mirror)

        def keep_block(inner):
            return inner
        return (lax.cond(weight > 0.0, apply_block, keep_block, accum), None)
    start_value = jnp.zeros((total, BS, K), jnp.float32)
    accum, _ = lax.scan(add_block, start_value, (flat_blocks, flat_rows, flat_cols, weights))
    products = accum.reshape(total * BS, K)
    gram = jnp.dot(products.T.astype(jnp.float32), products.astype(jnp.float32), precision=lax.Precision.HIGHEST, preferred_element_type=jnp.float32) / (total * BS)
    lower = jnp.linalg.cholesky(gram)
    basis = jax.scipy.linalg.solve_triangular(lower, products.T, lower=True).T
    return (basis, lower.T)
```

```python
import functools

import jax
import jax.numpy as jnp
from jax import lax
from jax.experimental import pallas as pl
from jax.experimental.pallas import tpu as pltpu
from jax.sharding import PartitionSpec as P

CORES = 2
DEPTH = 4
PANEL = 32
GROUP = 8
MESH = pl.DeviceIdType.MESH
HIGHEST = lax.Precision.HIGHEST


def products_kernel(
    n_row, n_col, slot_ref, weight_ref, blocks_ref, trials_ref, products_ref, gram_ref,
    row_vec, col_vec, dense, col_part, core_in, side_in, line_in, row_part, col_in,
    gram_part, gram_core, gram_mid, gram_col, gram_all,
    s_vec, r_vec, s_line, r_line, s_side, r_side, s_core, r_core,
    s_pc, r_pc, s_ps, r_ps, s_pl, r_pl, s_pr, r_pr,
    s_gc, r_gc, s_gm, r_gm, s_gy, r_gy, s_ga, r_ga, s_gb, r_gb,
):
    width = n_row // (CORES * DEPTH)
    mids = n_row // CORES
    edge, span = trials_ref.shape
    r, c = lax.axis_index("row"), lax.axis_index("col")
    z, x, k = r // (width * CORES), (r // CORES) % width, r % CORES
    mid = r // CORES
    other = 1 - k

    def at(zz, xx, kk):
        return ((zz * width + xx) * CORES + kk, c)

    core_peer = at(z, x, other)
    mid_peers = [((mid + d) % mids * CORES + k, c) for d in range(1, mids)]
    col_peers = [(r, (c + d) % n_col) for d in range(1, n_col)]

    barrier = pltpu.get_barrier_semaphore()
    for peer in [core_peer, *mid_peers, *col_peers]:
        pl.semaphore_signal(barrier, inc=1, device_id=peer, device_id_type=MESH)
    pl.semaphore_wait(barrier, 1 + len(mid_peers) + len(col_peers))

    def send(src, dst, s_sem, r_sem, peer):
        copy = pltpu.make_async_remote_copy(
            src_ref=src, dst_ref=dst, send_sem=s_sem, recv_sem=r_sem,
            device_id=peer, device_id_type=MESH,
        )
        copy.start()
        return copy

    done = []
    vec_copies = [
        send(trials_ref, row_vec.at[c], s_vec.at[d], r_vec.at[d], peer)
        for d, peer in enumerate(col_peers)
    ]
    line_copies = [
        send(trials_ref, col_vec.at[z, x, k], s_line.at[d - 1], r_line.at[d - 1], at((z + d) % DEPTH, x, k))
        for d in range(1, DEPTH)
    ]
    row_vec[c] = trials_ref[...]
    col_vec[z, x, k] = trials_ref[...]

    def place_cells(b, carry):
        for a in range(n_col):
            cell = a * n_row + b
            w = blocks_ref[slot_ref[cell]].astype(jnp.float32) * weight_ref[cell]
            dense[b, a * edge:(a + 1) * edge, :] = w.astype(jnp.bfloat16)
        return carry

    lax.fori_loop(0, n_row, place_cells, 0)

    for copy in vec_copies:
        copy.wait()
    vectors = row_vec[...].reshape(n_col * edge, span)

    def mirror(zz, xx, kk):
        b = (zz * width + xx) * CORES + kk
        col_part[zz, xx, kk] = lax.dot_general(
            dense[b], vectors, (((0,), (0,)), ((), ())), preferred_element_type=jnp.float32
        )

    order = [(z + 1 + t) % DEPTH for t in range(DEPTH)]
    core_copies = []
    for t in range(DEPTH):
        for xx in range(width):
            mirror(order[t], xx, other)
        core_copies.append(
            send(col_part.at[order[t], :, other], core_in.at[order[t]], s_pc.at[t], r_pc.at[t], core_peer)
        )
    for t in range(DEPTH):
        for xx in range(width):
            mirror(order[t], xx, k)

    for copy in line_copies:
        copy.wait()

    side_copies = []
    for t in range(DEPTH):
        zz = order[t]
        core_copies[t].wait()
        for xx in range(width):
            core_in[zz, xx] = core_in[zz, xx] + col_part[zz, xx, k]
        side_copies.append([
            send(core_in.at[zz, (x + d) % width], side_in.at[d - 1, zz], s_ps.at[t, d - 1], r_ps.at[t, d - 1],
                 at(z, (x + d) % width, k))
            for d in range(1, width)
        ])
    vec_side = [
        send(col_vec.at[:, x, k], col_vec.at[:, x, k], s_side.at[d - 1], r_side.at[d - 1], at(z, (x + d) % width, k))
        for d in range(1, width)
    ]
    tail_copies = []
    for t in range(DEPTH):
        zz = order[t]
        for copy in side_copies[t]:
            copy.wait()
        total = core_in[zz, x]
        for d in range(1, width):
            total = total + side_in[d - 1, zz]
        side_in[0, zz] = total
        if t < DEPTH - 1:
            tail_copies.append(
                send(side_in.at[0, zz], line_in.at[t], s_pl.at[t], r_pl.at[t], at(zz, x, k))
            )
    for copy in vec_side:
        copy.wait()
    vec_core = send(col_vec.at[:, :, k], col_vec.at[:, :, k], s_core, r_core, core_peer)
    vec_core.wait()

    row_part[...] = jnp.zeros_like(row_part)

    def direct(b, carry):
        zz, xx, kk = b // (width * CORES), (b // CORES) % width, b % CORES
        row_part[...] += jnp.dot(
            dense[b], col_vec[zz, xx, kk], preferred_element_type=jnp.float32
        ).reshape(row_part.shape)
        return carry

    lax.fori_loop(0, n_row, direct, 0)
    row_copies = [
        send(row_part.at[(c + d) % n_col], col_in.at[d - 1], s_pr.at[d - 1], r_pr.at[d - 1], col_peers[d - 1])
        for d in range(1, n_col)
    ]
    for copy in tail_copies:
        copy.wait()
    total = side_in[0, z] + row_part[c]
    for d in range(DEPTH - 1):
        total = total + line_in[d]
    for copy in row_copies:
        copy.wait()
    for d in range(n_col - 1):
        total = total + col_in[d]
    products_ref[...] = total

    half, piece = span // CORES, span // n_row
    gram_part[...] = lax.dot_general(
        total, total, (((0,), (0,)), ((), ())), precision=HIGHEST, preferred_element_type=jnp.float32
    ) * (1.0 / (n_row * n_col * edge))
    send(
        gram_part.at[pl.ds(pl.multiple_of(other * half, half), half)], gram_core, s_gc, r_gc, core_peer
    ).wait()
    mine = pl.ds(pl.multiple_of(k * half, half), half)
    gram_core[...] = gram_core[...] + gram_part[mine]

    def rows_of(m):
        return pl.ds(pl.multiple_of(m * piece, piece), piece)

    mid_copies = [
        send(gram_core.at[rows_of((mid + d) % mids)], gram_mid.at[d - 1], s_gm.at[d - 1], r_gm.at[d - 1], mid_peers[d - 1])
        for d in range(1, mids)
    ]
    total = gram_core[rows_of(mid)]
    for d in range(1, mids):
        mid_copies[d - 1].wait()
        total = total + gram_mid[d - 1]
    gram_col[c] = total
    col_copies = [
        send(gram_col.at[c], gram_col.at[c], s_gy.at[d - 1], r_gy.at[d - 1], col_peers[d - 1])
        for d in range(1, n_col)
    ]
    for copy in col_copies:
        copy.wait()
    total = gram_col[0]
    for d in range(1, n_col):
        total = total + gram_col[d]
    own = pl.ds(pl.multiple_of(k * half + mid * piece, piece), piece)
    gram_all[own] = total
    back = [
        send(gram_all.at[own], gram_all.at[own], s_ga.at[d - 1], r_ga.at[d - 1], mid_peers[d - 1])
        for d in range(1, mids)
    ]
    for copy in back:
        copy.wait()
    send(gram_all.at[mine], gram_all.at[mine], s_gb, r_gb, core_peer).wait()
    gram_ref[...] = gram_all[...]


def factor_kernel(gram_ref, products_ref, basis_ref, factor_ref, work):
    span = gram_ref.shape[0]
    rows_all = lax.broadcasted_iota(jnp.int32, (span, span), 0)
    cols_all = lax.broadcasted_iota(jnp.int32, (span, span), 1)
    work[:, :span] = gram_ref[...]
    work[:, span:] = jnp.where(rows_all == cols_all, 1.0, 0.0).astype(jnp.float32)
    place = lax.broadcasted_iota(jnp.int32, (PANEL, 128), 0)
    tiles = 2 * span // 128
    for first in range(0, span, PANEL):
        base = first // 128 * 128
        last_tile = (span + first + PANEL + 127) // 128
        live = [t for t in range(tiles) if first // 128 <= t < last_tile]
        part = {t: work[first:first + PANEL, t * 128:(t + 1) * 128] for t in live}
        scale = jnp.ones((PANEL, 128), jnp.float32)
        for start in range(0, PANEL, GROUP):
            lane = first + start - base
            lead = part[first // 128]
            cols = [
                jnp.broadcast_to(lead[:, lane + m:lane + m + 1], (PANEL, 128)) for m in range(GROUP)
            ]
            for m in range(GROUP):
                at = start + m
                pivot = cols[m][at:at + 1]
                root = lax.rsqrt(pivot)
                root = root * (1.5 - 0.5 * pivot * root * root)
                inverse = root * root
                below = jnp.where(place > at, cols[m], 0.0)
                for other in range(m + 1, GROUP):
                    cols[other] = cols[other] - below * (cols[other][at:at + 1] * inverse)
                for t in live:
                    part[t] = part[t] - below * (part[t][at:at + 1] * inverse)
                scale = jnp.where(place == at, root, scale)
        for t in live:
            part[t] = part[t] * scale
            work[first:first + PANEL, t * 128:(t + 1) * 128] = part[t]
        after = first + PANEL
        if after < span:
            low = after // 128
            left = jnp.concatenate([part[t] for t in range(low, span // 128)], axis=1)
            right = jnp.concatenate([part[t] for t in range(low, last_tile)], axis=1)
            change = lax.dot_general(
                left, right, (((0,), (0,)), ((), ())), precision=HIGHEST, preferred_element_type=jnp.float32
            )
            work[after:, low * 128:last_tile * 128] -= change[after - low * 128:]
    factor_ref[...] = jnp.where(rows_all <= cols_all, work[:, :span], 0.0)
    basis_ref[...] = lax.dot_general(
        products_ref[...], work[:, span:], (((1,), (1,)), ((), ())),
        precision=HIGHEST, preferred_element_type=jnp.float32,
    )


def body(blocks, block_rows, block_cols, counts, trials):
    n_row, n_col = lax.axis_size("row"), lax.axis_size("col")
    width, mids = n_row // (CORES * DEPTH), n_row // CORES
    edge, span = trials.shape
    row_index, col_index = block_rows[0], block_cols[0]
    cells = n_row * n_col
    slots = row_index.shape[0]
    spots = row_index // n_row * n_row + col_index % n_row
    position = jnp.arange(slots, dtype=jnp.int32)
    held = (spots[None, :] == jnp.arange(cells, dtype=jnp.int32)[:, None]) & (position < counts[0, 0])[None, :]
    slot = jnp.sum(jnp.where(held, position[None, :], 0), axis=1)
    weight = jnp.sum(
        jnp.where(held, jnp.where(row_index == col_index, 0.5, 1.0)[None, :], 0.0), axis=1
    ).astype(jnp.float32)

    vmem = pl.BlockSpec(memory_space=pltpu.VMEM)
    smem = pl.BlockSpec(memory_space=pltpu.SMEM)
    f32, bf16 = jnp.float32, jnp.bfloat16
    dma = pltpu.SemaphoreType.DMA
    side = max(width - 1, 1)

    def pair(shape=()):
        return [dma(shape) if shape else dma, dma(shape) if shape else dma]

    products, gram = pl.pallas_call(
        functools.partial(products_kernel, n_row, n_col),
        out_shape=(
            jax.ShapeDtypeStruct((edge, span), f32),
            jax.ShapeDtypeStruct((span, span), f32),
        ),
        in_specs=[smem, smem, vmem, vmem],
        out_specs=(vmem, vmem),
        scratch_shapes=[
            pltpu.VMEM((n_col, edge, span), bf16),
            pltpu.VMEM((DEPTH, width, CORES, edge, span), bf16),
            pltpu.VMEM((n_row, n_col * edge, edge), bf16),
            pltpu.VMEM((DEPTH, width, CORES, edge, span), f32),
            pltpu.VMEM((DEPTH, width, edge, span), f32),
            pltpu.VMEM((side, DEPTH, edge, span), f32),
            pltpu.VMEM((DEPTH - 1, edge, span), f32),
            pltpu.VMEM((n_col, edge, span), f32),
            pltpu.VMEM((n_col - 1, edge, span), f32),
            pltpu.VMEM((span, span), f32),
            pltpu.VMEM((span // CORES, span), f32),
            pltpu.VMEM((mids - 1, span // n_row, span), f32),
            pltpu.VMEM((n_col, span // n_row, span), f32),
            pltpu.VMEM((span, span), f32),
            *pair((n_col - 1,)), *pair((DEPTH - 1,)), *pair((side,)), *pair(),
            *pair((DEPTH,)), *pair((DEPTH, side)), *pair((DEPTH - 1,)), *pair((n_col - 1,)),
            *pair(), *pair((mids - 1,)), *pair((n_col - 1,)), *pair((mids - 1,)), *pair(),
        ],
        compiler_params=pltpu.CompilerParams(
            collective_id=0, has_side_effects=True, vmem_limit_bytes=48 * 1024 * 1024
        ),
        name="products",
    )(slot, weight, blocks[0], trials)

    basis, factor = pl.pallas_call(
        factor_kernel,
        out_shape=(
            jax.ShapeDtypeStruct((edge, span), f32),
            jax.ShapeDtypeStruct((span, span), f32),
        ),
        in_specs=[vmem, vmem],
        out_specs=(vmem, vmem),
        scratch_shapes=[pltpu.VMEM((span, 2 * span), f32)],
        compiler_params=pltpu.CompilerParams(vmem_limit_bytes=32 * 1024 * 1024),
        name="factorize",
    )(gram, products)
    return basis, factor


def solution(mesh):
    return jax.shard_map(
        body,
        mesh=mesh,
        in_specs=(
            P("row", "col", None, None),
            P("row", "col"),
            P("row", "col"),
            P("row", "col"),
            P(("col", "row"), None),
        ),
        out_specs=(P(("col", "row"), None), P()),
        check_vma=False,
    )
```

```python
import functools

import jax
import jax.numpy as jnp
from jax import lax
from jax.experimental import pallas as pl
from jax.experimental.pallas import tpu as pltpu
from jax.sharding import PartitionSpec as P

CORES = 2
DEPTH = 4
PANEL = 32
GROUP = 8
MESH = pl.DeviceIdType.MESH
HIGHEST = lax.Precision.HIGHEST


def products_kernel(
    n_row, n_col, info_ref, blocks_ref, trials_ref, products_ref, gram_ref,
    held, row_vec, col_vec, dense, col_part, core_in, side_in, line_in, row_part, col_in,
    gram_part, gram_core, gram_mid, gram_col, gram_all, held_sem,
    s_vec, r_vec, s_line, r_line, s_side, r_side, s_core, r_core,
    s_pc, r_pc, s_ps, r_ps, s_pl, r_pl, s_pr, r_pr,
    s_gc, r_gc, s_gm, r_gm, s_gy, r_gy, s_ga, r_ga, s_gb, r_gb,
):
    width = n_row // (CORES * DEPTH)
    mids = n_row // CORES
    cells = n_row * n_col
    edge, span = trials_ref.shape
    load = pltpu.make_async_copy(blocks_ref, held, held_sem)
    load.start()
    r, c = lax.axis_index("row"), lax.axis_index("col")
    z, x, k = r // (width * CORES), (r // CORES) % width, r % CORES
    mid = r // CORES
    other = 1 - k

    def at(zz, xx, kk):
        return ((zz * width + xx) * CORES + kk, c)

    core_peer = at(z, x, other)
    mid_peers = [((mid + d) % mids * CORES + k, c) for d in range(1, mids)]
    col_peers = [(r, (c + d) % n_col) for d in range(1, n_col)]

    barrier = pltpu.get_barrier_semaphore()
    for peer in [core_peer, *mid_peers, *col_peers]:
        pl.semaphore_signal(barrier, inc=1, device_id=peer, device_id_type=MESH)

    def columns(b):
        return pl.ds(pl.multiple_of(b * edge, edge), edge)

    def place_cells(b, carry):
        for a in range(n_col):
            cell = a * n_row + b
            weight = info_ref[cells + cell].astype(jnp.float32) * 0.5
            w = held[info_ref[cell]].astype(jnp.float32) * weight
            dense[a * edge:(a + 1) * edge, columns(b)] = w.astype(jnp.bfloat16)
        return carry

    load.wait()
    lax.fori_loop(0, n_row // 2, place_cells, 0)
    pl.semaphore_wait(barrier, 1 + len(mid_peers) + len(col_peers))

    def send(src, dst, s_sem, r_sem, peer):
        copy = pltpu.make_async_remote_copy(
            src_ref=src, dst_ref=dst, send_sem=s_sem, recv_sem=r_sem,
            device_id=peer, device_id_type=MESH,
        )
        copy.start()
        return copy

    vec_copies = [
        send(trials_ref, row_vec.at[c], s_vec.at[d], r_vec.at[d], peer)
        for d, peer in enumerate(col_peers)
    ]
    line_copies = [
        send(trials_ref, col_vec.at[z, x, k], s_line.at[d - 1], r_line.at[d - 1], at((z + d) % DEPTH, x, k))
        for d in range(1, DEPTH)
    ]
    row_vec[c] = trials_ref[...]
    col_vec[z, x, k] = trials_ref[...]
    lax.fori_loop(n_row // 2, n_row, place_cells, 0)

    for copy in vec_copies:
        copy.wait()
    vectors = row_vec[...].reshape(n_col * edge, span)

    def mirror(zz, xx, kk):
        b = (zz * width + xx) * CORES + kk
        col_part[zz, xx, kk] = lax.dot_general(
            dense[:, columns(b)], vectors, (((0,), (0,)), ((), ())), preferred_element_type=jnp.float32
        )

    order = [(z + 1 + t) % DEPTH for t in range(DEPTH)]
    core_copies = []
    for t in range(DEPTH):
        for xx in range(width):
            mirror(order[t], xx, other)
        core_copies.append(
            send(col_part.at[order[t], :, other], core_in.at[order[t]], s_pc.at[t], r_pc.at[t], core_peer)
        )
    for t in range(DEPTH):
        for xx in range(width):
            mirror(order[t], xx, k)

    side_copies = []
    for t in range(DEPTH):
        zz = order[t]
        core_copies[t].wait()
        for xx in range(width):
            core_in[zz, xx] = core_in[zz, xx] + col_part[zz, xx, k]
        side_copies.append([
            send(core_in.at[zz, (x + d) % width], side_in.at[d - 1, zz], s_ps.at[t, d - 1], r_ps.at[t, d - 1],
                 at(z, (x + d) % width, k))
            for d in range(1, width)
        ])
        if t == 0:
            for copy in line_copies:
                copy.wait()
            vec_side = [
                send(col_vec.at[:, x, k], col_vec.at[:, x, k], s_side.at[d - 1], r_side.at[d - 1],
                     at(z, (x + d) % width, k))
                for d in range(1, width)
            ]

    tail_copies = []
    for t in range(DEPTH):
        zz = order[t]
        for copy in side_copies[t]:
            copy.wait()
        total = core_in[zz, x]
        for d in range(1, width):
            total = total + side_in[d - 1, zz]
        side_in[0, zz] = total
        if t < DEPTH - 1:
            tail_copies.append(
                send(side_in.at[0, zz], line_in.at[t], s_pl.at[t], r_pl.at[t], at(zz, x, k))
            )
        if t == 0:
            for copy in vec_side:
                copy.wait()
            vec_core = send(col_vec.at[:, :, k], col_vec.at[:, :, k], s_core, r_core, core_peer)
        if t == 1:
            vec_core.wait()
            group = width * CORES * edge
            acc = jnp.zeros((n_col * edge, span), jnp.float32)
            for part in range(DEPTH):
                acc = acc + jnp.dot(
                    dense[:, part * group:(part + 1) * group], col_vec[part].reshape(group, span),
                    preferred_element_type=jnp.float32,
                )
            row_part[...] = acc.reshape(row_part.shape)
            row_copies = [
                send(row_part.at[(c + d) % n_col], col_in.at[d - 1], s_pr.at[d - 1], r_pr.at[d - 1], col_peers[d - 1])
                for d in range(1, n_col)
            ]
    total = side_in[0, z] + row_part[c]
    for copy in row_copies:
        copy.wait()
    for d in range(n_col - 1):
        total = total + col_in[d]
    for d in range(DEPTH - 1):
        tail_copies[d].wait()
        total = total + line_in[d]
    products_ref[...] = total

    quarter, piece = span // 2, gram_mid.shape[1]
    half = piece * mids
    left, right = total[:, :quarter], total[:, quarter:]

    def inner(a, b):
        return lax.dot_general(
            a, b, (((0,), (0,)), ((), ())), precision=HIGHEST, preferred_element_type=jnp.float32
        ) * (1.0 / (n_row * n_col * edge))

    if gram_part.shape[0] > 3 * quarter:
        gram_part[3 * quarter:] = jnp.zeros((gram_part.shape[0] - 3 * quarter, quarter), jnp.float32)
    gram_part[:quarter] = inner(left, left)
    gram_part[quarter:2 * quarter] = inner(left, right)
    gram_part[2 * quarter:3 * quarter] = inner(right, right)
    send(
        gram_part.at[pl.ds(pl.multiple_of(other * half, 8), half)], gram_core, s_gc, r_gc, core_peer
    ).wait()
    mine = pl.ds(pl.multiple_of(k * half, 8), half)
    gram_core[...] = gram_core[...] + gram_part[mine]

    def rows_of(m):
        return pl.ds(pl.multiple_of(m * piece, 8), piece)

    mid_copies = [
        send(gram_core.at[rows_of((mid + d) % mids)], gram_mid.at[d - 1], s_gm.at[d - 1], r_gm.at[d - 1], mid_peers[d - 1])
        for d in range(1, mids)
    ]
    total = gram_core[rows_of(mid)]
    for d in range(1, mids):
        mid_copies[d - 1].wait()
        total = total + gram_mid[d - 1]
    gram_col[c] = total
    col_copies = [
        send(gram_col.at[c], gram_col.at[c], s_gy.at[d - 1], r_gy.at[d - 1], col_peers[d - 1])
        for d in range(1, n_col)
    ]
    for copy in col_copies:
        copy.wait()
    total = gram_col[0]
    for d in range(1, n_col):
        total = total + gram_col[d]
    own = pl.ds(pl.multiple_of(k * half + mid * piece, 8), piece)
    gram_all[own] = total
    back = [
        send(gram_all.at[own], gram_all.at[own], s_ga.at[d - 1], r_ga.at[d - 1], mid_peers[d - 1])
        for d in range(1, mids)
    ]
    for copy in back:
        copy.wait()
    send(gram_all.at[mine], gram_all.at[mine], s_gb, r_gb, core_peer).wait()
    gram_ref[...] = gram_all[:3 * quarter]


def factor_kernel(gram_ref, products_ref, basis_ref, factor_ref, work):
    span = work.shape[0]
    rows_all = lax.broadcasted_iota(jnp.int32, (span, span), 0)
    cols_all = lax.broadcasted_iota(jnp.int32, (span, span), 1)
    quarter = span // 2
    work[:quarter, :quarter] = gram_ref[:quarter]
    work[:quarter, quarter:span] = gram_ref[quarter:span]
    work[quarter:, quarter:span] = gram_ref[span:]
    work[quarter:, :quarter] = jnp.zeros((quarter, quarter), jnp.float32)
    work[:, span:] = jnp.where(rows_all == cols_all, 1.0, 0.0).astype(jnp.float32)
    place = lax.broadcasted_iota(jnp.int32, (PANEL, 128), 0)
    tiles = 2 * span // 128
    for first in range(0, span, PANEL):
        base = first // 128 * 128
        last_tile = (span + first + PANEL + 127) // 128
        live = [t for t in range(tiles) if first // 128 <= t < last_tile]
        part = {t: work[first:first + PANEL, t * 128:(t + 1) * 128] for t in live}
        scale = jnp.ones((PANEL, 128), jnp.float32)
        for start in range(0, PANEL, GROUP):
            lane = first + start - base
            lead = part[first // 128]
            cols = [
                jnp.broadcast_to(lead[:, lane + m:lane + m + 1], (PANEL, 128)) for m in range(GROUP)
            ]
            for m in range(GROUP):
                at = start + m
                pivot = cols[m][at:at + 1]
                root = lax.rsqrt(pivot)
                root = root * (1.5 - 0.5 * pivot * root * root)
                inverse = root * root
                below = jnp.where(place > at, cols[m], 0.0)
                for other in range(m + 1, GROUP):
                    cols[other] = cols[other] - below * (cols[other][at:at + 1] * inverse)
                for t in live:
                    part[t] = part[t] - below * (part[t][at:at + 1] * inverse)
                scale = jnp.where(place == at, root, scale)
        for t in live:
            part[t] = part[t] * scale
            work[first:first + PANEL, t * 128:(t + 1) * 128] = part[t]
        after = first + PANEL
        if after < span:
            low = after // 128
            left = jnp.concatenate([part[t] for t in range(low, span // 128)], axis=1)
            right = jnp.concatenate([part[t] for t in range(low, last_tile)], axis=1)
            change = lax.dot_general(
                left, right, (((0,), (0,)), ((), ())), precision=HIGHEST, preferred_element_type=jnp.float32
            )
            work[after:, low * 128:last_tile * 128] -= change[after - low * 128:]
    factor_ref[...] = jnp.where(rows_all <= cols_all, work[:, :span], 0.0)
    basis_ref[...] = lax.dot_general(
        products_ref[...], work[:, span:], (((1,), (1,)), ((), ())),
        precision=HIGHEST, preferred_element_type=jnp.float32,
    )


def body(blocks, block_rows, block_cols, counts, trials):
    n_row, n_col = lax.axis_size("row"), lax.axis_size("col")
    width, mids = n_row // (CORES * DEPTH), n_row // CORES
    edge, span = trials.shape
    row_index, col_index = block_rows[0], block_cols[0]
    cells = n_row * n_col
    slots = row_index.shape[0]
    spots = row_index // n_row * n_row + col_index % n_row
    position = jnp.arange(slots, dtype=jnp.int32)
    held = (spots[None, :] == jnp.arange(cells, dtype=jnp.int32)[:, None]) & (position < counts[0, 0])[None, :]
    twice = jnp.where(row_index == col_index, 1, 2).astype(jnp.int32)
    marks = jnp.stack([position, twice])
    info = jnp.sum(jnp.where(held[None], marks[:, None, :], 0), axis=2).reshape(2 * cells)

    vmem = pl.BlockSpec(memory_space=pltpu.VMEM)
    smem = pl.BlockSpec(memory_space=pltpu.SMEM)
    f32, bf16 = jnp.float32, jnp.bfloat16
    dma = pltpu.SemaphoreType.DMA
    side = max(width - 1, 1)
    piece = (3 * span // 2 + 8 * n_row - 1) // (8 * n_row) * 8

    def pair(shape=()):
        return [dma(shape) if shape else dma, dma(shape) if shape else dma]

    products, gram = pl.pallas_call(
        functools.partial(products_kernel, n_row, n_col),
        out_shape=(
            jax.ShapeDtypeStruct((edge, span), f32),
            jax.ShapeDtypeStruct((3 * span // 2, span // 2), f32),
        ),
        in_specs=[smem, pl.BlockSpec(memory_space=pltpu.HBM), vmem],
        out_specs=(vmem, vmem),
        scratch_shapes=[
            pltpu.VMEM((slots, edge, edge), bf16),
            pltpu.VMEM((n_col, edge, span), bf16),
            pltpu.VMEM((DEPTH, width, CORES, edge, span), bf16),
            pltpu.VMEM((n_col * edge, n_row * edge), bf16),
            pltpu.VMEM((DEPTH, width, CORES, edge, span), f32),
            pltpu.VMEM((DEPTH, width, edge, span), f32),
            pltpu.VMEM((side, DEPTH, edge, span), f32),
            pltpu.VMEM((DEPTH - 1, edge, span), f32),
            pltpu.VMEM((n_col, edge, span), f32),
            pltpu.VMEM((n_col - 1, edge, span), f32),
            pltpu.VMEM((piece * n_row, span // 2), f32),
            pltpu.VMEM((piece * mids, span // 2), f32),
            pltpu.VMEM((mids - 1, piece, span // 2), f32),
            pltpu.VMEM((n_col, piece, span // 2), f32),
            pltpu.VMEM((piece * n_row, span // 2), f32),
            dma,
            *pair((n_col - 1,)), *pair((DEPTH - 1,)), *pair((side,)), *pair(),
            *pair((DEPTH,)), *pair((DEPTH, side)), *pair((DEPTH - 1,)), *pair((n_col - 1,)),
            *pair(), *pair((mids - 1,)), *pair((n_col - 1,)), *pair((mids - 1,)), *pair(),
        ],
        compiler_params=pltpu.CompilerParams(
            collective_id=0, has_side_effects=True, vmem_limit_bytes=60 * 1024 * 1024
        ),
        name="products",
    )(info, blocks[0], trials)

    basis, factor = pl.pallas_call(
        factor_kernel,
        out_shape=(
            jax.ShapeDtypeStruct((edge, span), f32),
            jax.ShapeDtypeStruct((span, span), f32),
        ),
        in_specs=[vmem, vmem],
        out_specs=(vmem, vmem),
        scratch_shapes=[pltpu.VMEM((span, 2 * span), f32)],
        compiler_params=pltpu.CompilerParams(vmem_limit_bytes=32 * 1024 * 1024),
        name="factorize",
    )(gram, products)
    return basis, factor


def solution(mesh):
    return jax.shard_map(
        body,
        mesh=mesh,
        in_specs=(
            P("row", "col", None, None),
            P("row", "col"),
            P("row", "col"),
            P("row", "col"),
            P(("col", "row"), None),
        ),
        out_specs=(P(("col", "row"), None), P()),
        check_vma=False,
    )
```
